32 devices in a mesh: groups: 2 (over y), expert: 4 (over z), dp: 2 (over x), tensor: 2 (over core).
Axes of the slice: x: 2, y: 2, z: 4, core: 2. Of those that a mesh axis runs over, the one named last changes fastest.
Arguments:
- x_res: bfloat16 [2, 256, 1440], P(None, ('groups', 'expert', 'dp')), parts along dimension 1, may hold values from -6 to 6
- query_new: bfloat16 [2, 256, 2048], P(None, ('groups', 'expert', 'dp'), 'tensor'), parts along dimension 1, may hold values from -8 to 8
- key_new: bfloat16 [2, 256, 256], P(None, ('groups', 'expert', 'dp'), 'tensor'), parts along dimension 1, may hold values from -6 to 6
- value_new: bfloat16 [2, 256, 256], P(None, ('groups', 'expert', 'dp'), 'tensor'), parts along dimension 1, may hold values from -6 to 6
- key_cache: bfloat16 [256, 64, 256], P(('groups', 'expert', 'dp'), None, 'tensor'), parts along dimension 0, may hold values from -8 to 8
- value_cache: bfloat16 [256, 64, 256], P(('groups', 'expert', 'dp'), None, 'tensor'), parts along dimension 0, may hold values from -6 to 6
- lengths: int32 [256], P(('groups', 'expert', 'dp')), parts along dimension 0, may hold values from 2 to 64, as said below
- routes: int32 [2, 256, 4], P(None, ('groups', 'expert', 'dp')), parts along dimension 1, may hold values from 0 to 7, all different within a row; in each aligned block of 16 rows (0 to 15, 16 to 31, ..., all dimensions but the last counted through in order) at most 16 rows name the same one
- route_weight: float32 [2, 256, 4], P(None, ('groups', 'expert', 'dp')), parts along dimension 1, may hold values from 0.2 to 1
- norm_gain: float32 [1440], replicated, may hold values from 0.1 to 1.9
- out_weight: bfloat16 [2048, 1440], P('tensor', 'dp'), may hold values from -0.125 to 0.125
- w_gate: bfloat16 [8, 1440, 1440], P(None, 'expert', ('dp', 'tensor')), may hold values from -0.15625 to 0.15625
- w_up: bfloat16 [8, 1440, 1440], P(None, 'expert', ('dp', 'tensor')), may hold values from -0.15625 to 0.15625
- w_down: bfloat16 [8, 1440, 1440], P(None, 'expert', ('dp', 'tensor')), may hold values from -0.15625 to 0.15625
Outputs:
- layer_out: bfloat16 [2, 256, 1440], P(None, ('groups', 'expert', 'dp'), 'tensor'), parts along dimension 1
The draws below stay inside these ranges and needn't reach their ends.
There are 2 independent parts, one for each index of `groups`. The reference program is written for one: setup_inputs(seed, part) draws one part's arguments, and reference() takes and returns one part's arrays. A program takes and returns all parts, laid end to end along the dimension named above; an argument that names none is the same for every part. Nothing has to cross between parts.
Inputs may be any that keep to these rules, and one draw needn't show every extreme that they name: `routes`: each token names 4 different experts. Within one step the 16 tokens of one device (an aligned block of rows) name any one expert at most 16 times, a bound that some block reaches. `lengths`: some sequence uses all 64 positions.
All inputs are finite; a program needn't handle non-finite values.
Results may differ from the reference program's by a relative error of at most 0.0054.
Values may be sent and summed in bfloat16 or wider, within the bound.
A program may use at most 128 MiB of HBM per device.

```python
import math
import jax
import jax.numpy as jnp
import numpy as np
from jax import lax

D = 1440
FF = 1440
EXPERTS = 8
TOP = 4
HEAD_DIM = 64
QW = 2048
KW = 256
TOK_DEV = 16
BATCH = 128
CACHE = 64
STEPS = 2
CAP = 16


def draw_query_new(key, part):
    key = jax.random.fold_in(key, 11)
    values = jnp.clip(jax.random.normal(key, (STEPS, BATCH, QW), jnp.float32), -6.0, 6.0)
    return values.astype(jnp.bfloat16)


def draw_key_cache(key, part):
    key = jax.random.fold_in(key, 12)
    values = jnp.clip(jax.random.normal(key, (BATCH, CACHE, KW), jnp.float32), -6.0, 6.0)
    return values.astype(jnp.bfloat16)


def draw_lengths(key, part):
    key = jax.random.fold_in(key, 13)
    value_key, spot_key = jax.random.split(key)
    values = jax.random.randint(value_key, (BATCH,), 2, CACHE + 1)
    spot = jax.random.randint(spot_key, (), 0, BATCH)
    return jnp.where(jnp.arange(BATCH) == spot, CACHE, values).astype(jnp.int32)


def levels(rng, extent, shards, low, top_value):
    level = 1.0
    for dim, shards_of in shards:
        steps = jax.random.uniform(jax.random.fold_in(jax.random.fold_in(rng, 6), dim), (shards_of,), jnp.float32, low / len(shards), top_value / len(shards))
        level = level * jnp.repeat(jnp.exp(steps), extent[dim] // shards_of).reshape((-1,) + (1,) * (len(extent) - 1 - dim))
    return level


def routed_block(stream_key, own, number, rows, amount, top, bound, slope):
    sequence = jax.random.permutation(stream_key, amount)
    heavy_load, common = portions_of(amount, rows * top, bound, slope, True), portions_of(amount, rows * top, bound, slope, False)
    places = jnp.arange(amount)

    def named(sizes, rotation):
        used = int((sizes > 0).sum())
        fixed = max(1, used // 4)
        moved = fixed + (places - fixed + rotation * (used - fixed)) % max(1, amount - fixed)
        return jnp.zeros((amount,), jnp.int32).at[sequence[jnp.where(places < fixed, places, moved)]].set(jnp.asarray(sizes, jnp.int32))

    sizes = jnp.where(number % 4 == 0, named(heavy_load, number // 4), named(common, number - number // 4 - 1))
    mixed = jax.random.permutation(jax.random.fold_in(own, 3), amount)
    source_of, taker = mixed[0:amount // 2 * 2:2], mixed[1:amount // 2 * 2:2]
    slack = jnp.minimum(sizes[source_of] - 1, bound - sizes[taker]) // 2
    slack = jnp.where((source_of == sequence[0]) | (taker == sequence[0]) | (sizes[taker] == 0), 0, jnp.maximum(slack, 0))
    moved = jax.random.randint(jax.random.fold_in(own, 4), (amount // 2,), 0, 1 << 20) % (slack + 1)
    sizes = sizes.at[source_of].add(-moved).at[taker].add(moved)
    labels = jnp.searchsorted(jnp.cumsum(sizes), jnp.arange(rows * top), side="right").astype(jnp.int32)
    listing = labels.reshape(top, rows).T
    listing = listing[jax.random.permutation(jax.random.fold_in(own, 1), rows)]
    rotation = jax.random.randint(jax.random.fold_in(own, 2), (rows, 1), 0, top)
    return jnp.take_along_axis(listing, (jnp.arange(top)[None, :] + rotation) % top, axis=1)


def portions_of(count, total, bound, skew, full):
    loads = [(1 << 20) // math.isqrt(grade ** skew) + 1 for grade in range(1, count + 1)]
    largest = bound if full else min(bound, max(-(-total // count), total * loads[0] // sum(loads)))
    least = 1 if total - largest >= count - 1 else 0
    holding, surplus = [largest] + [least] * (count - 1), total - largest - least * (count - 1)
    while surplus > 0:
        free = [i for i in range(1, count) if holding[i] < largest] or [i for i in range(1, count) if holding[i] < bound]
        whole, remaining = sum([loads[i] for i in free]), surplus
        for i in free:
            extra = min(bound - holding[i], max(1, remaining * loads[i] // whole), surplus)
            holding[i] = holding[i] + extra
            surplus = surplus - extra
    return np.array(holding)


def normal_values(stream_key, shape, scale, most, shards=(), kind=jnp.bfloat16):
    drawn = jax.random.normal(stream_key, shape, jnp.float32) * scale
    if len(shards) > 0:
        drawn = levels(stream_key, shape, shards, -0.22, 0.18) * drawn
    return jnp.clip(drawn, min=-most, max=most).astype(kind)


def setup_inputs(seed: int = 0, part: int = 0) -> dict:
    arg_keys = jax.random.split(jax.random.key(seed), 15)
    part_keys = jax.random.split(jax.random.fold_in(arg_keys[14], part), 15)
    x_res = normal_values(part_keys[0], (STEPS, BATCH, D), 1.0, 6.0, ((1, 8),))
    query_new = draw_query_new(jax.random.fold_in(jax.random.fold_in(arg_keys[14], part), 71), part)
    key_new = normal_values(part_keys[2], (STEPS, BATCH, KW), 1.0, 6.0, ((1, 8), (2, 2)))
    value_new = normal_values(part_keys[3], (STEPS, BATCH, KW), 1.0, 6.0, ((1, 8), (2, 2)))
    key_cache = draw_key_cache(jax.random.fold_in(jax.random.fold_in(arg_keys[14], part), 71), part)
    value_cache = normal_values(part_keys[5], (BATCH, CACHE, KW), 1.0, 6.0, ((0, 8), (2, 2)))
    lengths = draw_lengths(jax.random.fold_in(jax.random.fold_in(arg_keys[14], part), 71), part)
    routes_keys = jax.random.split(jax.random.fold_in(part_keys[7], 1), STEPS * BATCH // TOK_DEV)
    routes_turns = jax.random.permutation(jax.random.fold_in(part_keys[7], 3), STEPS * BATCH // TOK_DEV)
    routes = jax.vmap(lambda own, number: routed_block(jax.random.fold_in(part_keys[7], 2), own, number, TOK_DEV, EXPERTS, TOP, CAP, 2))(routes_keys, routes_turns).reshape((STEPS, BATCH, TOP))
    route_weight = jnp.clip(0.2 + 0.8 * jax.random.uniform(part_keys[8], (STEPS, BATCH, TOP), jnp.float32) ** levels(part_keys[8], (STEPS, BATCH, TOP), ((1, 8),), -0.2, 0.2), 0.2, 1.0)
    norm_gain = jnp.clip(1.0 + 0.18 * jax.random.normal(arg_keys[9], (D,), jnp.float32), 0.1, 1.9)
    out_weight = normal_values(arg_keys[10], (QW, D), QW ** -0.5, 0.125, ((0, 2), (1, 2)))
    w_gate = normal_values(arg_keys[11], (EXPERTS, D, FF), D ** -0.5, 0.15625, ((1, 4), (2, 4)))
    w_up = normal_values(arg_keys[12], (EXPERTS, D, FF), D ** -0.5, 0.15625, ((1, 4), (2, 4)))
    w_down = normal_values(arg_keys[13], (EXPERTS, D, FF), FF ** -0.5, 0.15625, ((1, 4), (2, 4)))
    return dict(x_res=x_res, query_new=query_new, key_new=key_new, value_new=value_new, key_cache=key_cache, value_cache=value_cache, lengths=lengths, routes=routes, route_weight=route_weight, norm_gain=norm_gain, out_weight=out_weight, w_gate=w_gate, w_up=w_up, w_down=w_down)


def attend(query_row, key_cache, value_cache, key_new, value_new, lengths, moment):
    batch_size = query_row.shape[0]
    groups = key_cache.shape[2] // HEAD_DIM
    per_group = query_row.shape[1] // (groups * HEAD_DIM)
    window = key_cache.shape[1]
    new_count = key_new.shape[0]
    queries = query_row.astype(jnp.float32).reshape(batch_size, groups, per_group, HEAD_DIM)
    old_keys = key_cache.astype(jnp.float32).reshape(batch_size, window, groups, HEAD_DIM)
    old_values = value_cache.astype(jnp.float32).reshape(batch_size, window, groups, HEAD_DIM)
    new_keys = key_new.astype(jnp.float32).reshape(new_count, batch_size, groups, HEAD_DIM)
    new_values = value_new.astype(jnp.float32).reshape(new_count, batch_size, groups, HEAD_DIM)
    factor = HEAD_DIM ** (-0.5)
    old_scores = jnp.einsum('bgrd,bcgd->bgrc', queries, old_keys) * factor
    new_scores = jnp.einsum('bgrd,sbgd->bgrs', queries, new_keys) * factor
    old_valid = (jnp.arange(window)[None, :] < lengths[:, None])[:, None, None, :]
    new_valid = (jnp.arange(new_count) <= moment)[None, None, None, :]
    scores = jnp.concatenate([jnp.where(old_valid, old_scores, -jnp.inf), jnp.where(new_valid, new_scores, -jnp.inf)], axis=-1)
    highest = lax.optimization_barrier(jnp.max(scores, axis=-1, keepdims=True))
    powers = jnp.exp(scores - highest)
    weights = (powers / lax.optimization_barrier(jnp.sum(powers, axis=-1, keepdims=True))).astype(jnp.bfloat16).astype(jnp.float32)
    attended = jnp.einsum('bgrc,bcgd->bgrd', weights[..., :window], old_values)
    attended = attended + jnp.einsum('bgrs,sbgd->bgrd', weights[..., window:], new_values)
    return attended.reshape(batch_size, groups * per_group * HEAD_DIM).astype(jnp.bfloat16)

def expert_block(slab):
    buffer, gate_matrix, up_matrix, down_matrix = slab
    gate_act = jnp.dot(buffer, gate_matrix, preferred_element_type=jnp.float32)
    up_act = jnp.dot(buffer, up_matrix, preferred_element_type=jnp.float32)
    activated = (jax.nn.silu(gate_act) * up_act).astype(jnp.bfloat16)
    return jnp.dot(activated, down_matrix.T, preferred_element_type=jnp.float32).astype(jnp.bfloat16)

def reference(x_res, query_new, key_new, value_new, key_cache, value_cache, lengths, routes, route_weight, norm_gain, out_weight, w_gate, w_up, w_down):
    room = BATCH // TOK_DEV * CAP
    results = []
    for moment in range(STEPS):
        attended = attend(query_new[moment], key_cache, value_cache, key_new, value_new, lengths, moment)
        hidden_state = x_res[moment].astype(jnp.float32) + jnp.dot(attended, out_weight, preferred_element_type=jnp.float32)
        mean_square = lax.optimization_barrier(jnp.mean(hidden_state * hidden_state, axis=-1, keepdims=True))
        normed = (hidden_state * lax.rsqrt(mean_square + 1e-05) * norm_gain).astype(jnp.bfloat16)
        chosen = routes[moment].reshape(-1).astype(jnp.int32)
        matches = (chosen[:, None] == jnp.arange(EXPERTS, dtype=jnp.int32)[None, :]).astype(jnp.int32)
        before = jnp.cumsum(matches, axis=0) - matches
        order_rank = lax.optimization_barrier(jnp.sum(before * matches, axis=1)).astype(jnp.int32)
        buffer = jnp.zeros((EXPERTS, room, D), jnp.bfloat16).at[chosen, order_rank].set(jnp.repeat(normed, TOP, axis=0))
        outputs = lax.map(expert_block, (buffer, w_gate, w_up, w_down))
        picked = outputs[chosen, order_rank].astype(jnp.float32).reshape(BATCH, TOP, D)
        combined = lax.optimization_barrier(jnp.sum(route_weight[moment][:, :, None] * picked, axis=1))
        results.append((hidden_state + combined).astype(jnp.bfloat16))
    return jnp.stack(results)
```

```python
import jax
import jax.numpy as jnp
from jax import lax
from jax.sharding import PartitionSpec as P

HEAD_DIM = 64


def attend(query_row, key_cache, value_cache, key_new, value_new, lengths, moment):
    batch_size = query_row.shape[0]
    groups = key_cache.shape[2] // HEAD_DIM
    per_group = query_row.shape[1] // (groups * HEAD_DIM)
    window = key_cache.shape[1]
    new_count = key_new.shape[0]
    queries = query_row.reshape(batch_size, groups, per_group, HEAD_DIM)
    old_keys = key_cache.reshape(batch_size, window, groups, HEAD_DIM)
    old_values = value_cache.reshape(batch_size, window, groups, HEAD_DIM)
    new_keys = key_new.reshape(new_count, batch_size, groups, HEAD_DIM)
    new_values = value_new.reshape(new_count, batch_size, groups, HEAD_DIM)
    factor = HEAD_DIM ** (-0.5)
    old_scores = (
        jnp.einsum("bgrd,bcgd->bgrc", queries, old_keys, preferred_element_type=jnp.float32)
        * factor
    )
    new_scores = (
        jnp.einsum("bgrd,sbgd->bgrs", queries, new_keys, preferred_element_type=jnp.float32)
        * factor
    )
    old_valid = (jnp.arange(window)[None, :] < lengths[:, None])[:, None, None, :]
    new_valid = (jnp.arange(new_count) <= moment)[None, None, None, :]
    scores = jnp.concatenate(
        [jnp.where(old_valid, old_scores, -jnp.inf), jnp.where(new_valid, new_scores, -jnp.inf)],
        axis=-1,
    )
    highest = jnp.max(scores, axis=-1, keepdims=True)
    powers = jnp.exp(scores - highest)
    weights = (powers / jnp.sum(powers, axis=-1, keepdims=True)).astype(jnp.bfloat16)
    attended = jnp.einsum(
        "bgrc,bcgd->bgrd", weights[..., :window], old_values, preferred_element_type=jnp.float32
    )
    attended = attended + jnp.einsum(
        "bgrs,sbgd->bgrd", weights[..., window:], new_values, preferred_element_type=jnp.float32
    )
    return attended.reshape(batch_size, groups * per_group * HEAD_DIM).astype(jnp.bfloat16)


def move_weights(
    x_res,
    query_new,
    key_new,
    value_new,
    key_cache,
    value_cache,
    lengths,
    routes,
    route_weight,
    norm_gain,
    out_weight,
    w_gate,
    w_up,
    w_down,
):
    expert_count = lax.axis_size("expert")
    row_count = lax.axis_size("dp")
    half_count = lax.axis_size("tensor")
    total_experts = w_gate.shape[0]
    owned_count = total_experts // expert_count
    copies = row_count // owned_count
    tokens = x_res.shape[1]
    choose_k = routes.shape[2]
    capacity = 2 * max(1, tokens * choose_k // total_experts)
    slot_count = capacity // copies
    width = x_res.shape[2]
    row_part = w_gate.shape[1]
    col_part = w_gate.shape[2]
    sectioned = tuple(
        (
            matrix.reshape(expert_count, owned_count, row_part, col_part)
            for matrix in (w_gate, w_up, w_down)
        )
    )
    doubled = tuple((jnp.repeat(matrix, copies, axis=1) for matrix in sectioned))
    placed = (
        lax.all_to_all(
            lax.all_to_all(doubled[0], "expert", split_axis=0, concat_axis=2, tiled=True),
            "dp",
            split_axis=1,
            concat_axis=3,
            tiled=True,
        ),
        lax.all_to_all(
            lax.all_to_all(doubled[1], "expert", split_axis=0, concat_axis=2, tiled=True),
            "dp",
            split_axis=1,
            concat_axis=3,
            tiled=True,
        ),
        lax.all_to_all(
            lax.all_to_all(doubled[2], "expert", split_axis=0, concat_axis=2, tiled=True),
            "dp",
            split_axis=1,
            concat_axis=3,
            tiled=True,
        ),
    )
    gate_w, up_w, down_w = (matrix.reshape(width, -1) for matrix in placed)
    out_proj = lax.all_gather(out_weight, "dp", axis=1, tiled=True)
    lane_ids = jnp.arange(expert_count * row_count * slot_count, dtype=jnp.int32)
    half_width = width // half_count
    results = []
    for moment in range(query_new.shape[0]):
        attended = attend(
            query_new[moment], key_cache, value_cache, key_new, value_new, lengths, moment
        )
        partial_value = jnp.dot(attended, out_proj, preferred_element_type=jnp.float32)
        hidden_state = x_res[moment].astype(jnp.float32) + lax.psum(partial_value, "tensor")
        mean_square = jnp.mean(hidden_state * hidden_state, axis=-1, keepdims=True)
        normed = (hidden_state * lax.rsqrt(mean_square + 1e-05) * norm_gain).astype(jnp.bfloat16)
        chosen = routes[moment].reshape(-1)
        matches = (chosen[:, None] == jnp.arange(total_experts, dtype=jnp.int32)[None, :]).astype(
            jnp.int32
        )
        before = jnp.cumsum(matches, axis=0) - matches
        order_rank = jnp.sum(before * matches, axis=1)
        target = (
            chosen // owned_count * row_count
            + chosen % owned_count * copies
            + order_rank // slot_count
        )
        lane_of = target * slot_count + order_rank % slot_count
        selector = lane_of[:, None] == lane_ids[None, :]
        per_token = jnp.any(selector.reshape(tokens, choose_k, -1), axis=1)
        outgoing = jnp.dot(
            per_token.T.astype(jnp.bfloat16), normed, preferred_element_type=jnp.float32
        ).astype(jnp.bfloat16)
        arrived = lax.all_to_all(
            outgoing.reshape(expert_count * row_count, slot_count, width),
            ("expert", "dp"),
            split_axis=0,
            concat_axis=0,
            tiled=True,
        )
        slot_rows = arrived.reshape(-1, width)
        gate_act = jnp.dot(slot_rows, gate_w, preferred_element_type=jnp.float32)
        up_act = jnp.dot(slot_rows, up_w, preferred_element_type=jnp.float32)
        activated = (jax.nn.silu(gate_act) * up_act).astype(jnp.bfloat16)
        partial_out = lax.dot_general(
            activated, down_w, (((1,), (1,)), ((), ())), preferred_element_type=jnp.float32
        )
        expert_out = lax.psum(partial_out, "tensor").astype(jnp.bfloat16)
        out_width = expert_out.shape[1]
        returned = lax.all_to_all(
            expert_out.reshape(expert_count * row_count, slot_count, out_width),
            ("expert", "dp"),
            split_axis=0,
            concat_axis=0,
            tiled=True,
        )
        gathered = jnp.dot(
            selector.astype(jnp.bfloat16),
            returned.reshape(-1, out_width),
            preferred_element_type=jnp.float32,
        )
        gathered = gathered.reshape(tokens, choose_k, out_width)
        combined = jnp.sum(route_weight[moment][:, :, None] * gathered, axis=1)
        whole_out = (hidden_state + combined).astype(jnp.bfloat16)
        results.append(
            lax.dynamic_slice_in_dim(
                whole_out, lax.axis_index("tensor") * half_width, half_width, 1
            )
        )
    return jnp.stack(results)


def attend_steps(query_new, key_cache, value_cache, key_new, value_new, lengths):
    steps, batch_size, query_width = query_new.shape
    groups = key_cache.shape[2] // HEAD_DIM
    per_group = query_width // (groups * HEAD_DIM)
    window = key_cache.shape[1]
    queries = query_new.reshape(steps, batch_size, groups, per_group, HEAD_DIM)
    queries = queries.transpose(1, 2, 0, 3, 4).reshape(
        batch_size, groups, steps * per_group, HEAD_DIM
    )
    keys = jnp.concatenate([key_cache, key_new.transpose(1, 0, 2)], axis=1)
    values = jnp.concatenate([value_cache, value_new.transpose(1, 0, 2)], axis=1)
    spots = window + steps
    keys = keys.reshape(batch_size, spots, groups, HEAD_DIM)
    values = values.reshape(batch_size, spots, groups, HEAD_DIM)
    scores = jnp.einsum("bgrd,bcgd->bgrc", queries, keys, preferred_element_type=jnp.float32)
    scores = scores * HEAD_DIM ** (-0.5)
    spot = jnp.arange(spots)[None, None, None, :]
    moment = (jnp.arange(steps * per_group) // per_group)[None, None, :, None]
    limit = lengths[:, None, None, None]
    valid = (spot < limit) | ((spot >= window) & (spot - window <= moment))
    scores = jnp.where(valid, scores, -jnp.inf)
    powers = jnp.exp(scores - jnp.max(scores, axis=-1, keepdims=True))
    probs = (powers / jnp.sum(powers, axis=-1, keepdims=True)).astype(jnp.bfloat16)
    attended = jnp.einsum("bgrc,bcgd->bgrd", probs, values, preferred_element_type=jnp.float32)
    attended = attended.astype(jnp.bfloat16).reshape(
        batch_size, groups, steps, per_group, HEAD_DIM
    )
    return attended.transpose(2, 0, 1, 3, 4).reshape(steps * batch_size, query_width)


def move_tokens(
    x_res,
    query_new,
    key_new,
    value_new,
    key_cache,
    value_cache,
    lengths,
    routes,
    route_weight,
    norm_gain,
    out_weight,
    w_gate,
    w_up,
    w_down,
):
    slices = lax.axis_size("expert")
    rows = lax.axis_size("dp")
    halves = lax.axis_size("tensor")
    experts, row_part, col_part = w_gate.shape
    steps, tokens, width = x_res.shape
    top = routes.shape[2]
    mine = steps * tokens
    block = mine // halves
    whole = mine * slices * rows
    everyone = ("expert", "dp", "tensor")

    packed = jnp.concatenate([routes.astype(jnp.float32), route_weight], axis=2)
    packed = lax.all_gather(packed.reshape(mine, 2 * top), ("expert", "dp"), axis=0, tiled=True)
    chosen = packed[:, :top].astype(jnp.int32)
    weight = packed[:, top:]

    attended = attend_steps(query_new, key_cache, value_cache, key_new, value_new, lengths)
    both = lax.all_gather(attended, "dp", axis=0, tiled=True)
    partial = jnp.dot(both, out_weight, preferred_element_type=jnp.float32)
    partial = lax.all_to_all(
        partial.reshape(rows * halves, block, -1),
        ("dp", "tensor"),
        split_axis=0,
        concat_axis=0,
        tiled=True,
    )
    projected = jnp.sum(partial.reshape(rows, halves, block, -1), axis=1)
    projected = projected.transpose(1, 0, 2).reshape(block, width)
    half = lax.axis_index("tensor")
    own = lax.dynamic_slice_in_dim(x_res.reshape(mine, width), half * block, block, 0)
    hidden_state = own.astype(jnp.float32) + projected
    mean_square = jnp.mean(hidden_state * hidden_state, axis=-1, keepdims=True)
    normed = (hidden_state * lax.rsqrt(mean_square + 1e-05) * norm_gain).astype(jnp.bfloat16)

    normed = lax.all_gather(normed, everyone, axis=0, tiled=True)
    place = lax.axis_index("expert")
    features = lax.dynamic_slice_in_dim(normed, place * row_part, row_part, 1)
    sums = []
    for matrix in (w_gate, w_up):
        dense = [
            jnp.dot(features, matrix[x], preferred_element_type=jnp.float32).astype(jnp.bfloat16)
            for x in range(experts)
        ]
        for k in range(top):
            value = dense[0]
            for x in range(1, experts):
                value = jnp.where(chosen[:, k : k + 1] == x, dense[x], value)
            sums.append(value.reshape(slices, whole // slices, col_part))
    sums = jnp.stack(sums, axis=1)
    sums = lax.psum_scatter(sums, "expert", scatter_dimension=0, tiled=True)[0]
    sums = sums.astype(jnp.float32)
    share = lax.dynamic_slice_in_dim(weight, place * (whole // slices), whole // slices, 0)
    activated = jax.nn.silu(sums[:top]) * sums[top:] * share.T[:, :, None]
    activated = lax.all_gather(activated.astype(jnp.bfloat16), "expert", axis=0)
    total = jnp.zeros((whole, row_part), jnp.float32)
    for x in range(experts):
        spread = jnp.zeros((whole, col_part), jnp.bfloat16)
        for k in range(top):
            spread = jnp.where(
                chosen[:, k : k + 1] == x, activated[:, k].reshape(whole, col_part), spread
            )
        total = total + lax.dot_general(
            spread, w_down[x], (((1,), (1,)), ((), ())), preferred_element_type=jnp.float32
        )
    returned = lax.all_to_all(
        total.reshape(slices * rows * halves, block, row_part),
        everyone,
        split_axis=0,
        concat_axis=0,
        tiled=True,
    )
    combined = jnp.sum(returned.reshape(slices, rows * halves, block, row_part), axis=1)
    combined = combined.transpose(1, 0, 2).reshape(block, width)
    result = (hidden_state + combined).astype(jnp.bfloat16).reshape(block, halves, width // halves)
    result = lax.all_to_all(
        result.transpose(1, 0, 2), "tensor", split_axis=0, concat_axis=0, tiled=True
    )
    return result.reshape(steps, tokens, width // halves)


def local(*args):
    x_res, routes, w_gate = args[0], args[7], args[11]
    spread = lax.axis_size("expert") * lax.axis_size("dp")
    travelling = x_res.shape[0] * x_res.shape[1] * spread * routes.shape[2]
    if travelling < w_gate.shape[0] * w_gate.shape[1]:
        return move_tokens(*args)
    return move_weights(*args)


def solution(mesh):
    in_specs = (
        P(None, ("groups", "expert", "dp"), None),
        P(None, ("groups", "expert", "dp"), "tensor"),
        P(None, ("groups", "expert", "dp"), "tensor"),
        P(None, ("groups", "expert", "dp"), "tensor"),
        P(("groups", "expert", "dp"), None, "tensor"),
        P(("groups", "expert", "dp"), None, "tensor"),
        P(("groups", "expert", "dp")),
        P(None, ("groups", "expert", "dp"), None),
        P(None, ("groups", "expert", "dp"), None),
        P(),
        P("tensor", "dp"),
        P(None, "expert", ("dp", "tensor")),
        P(None, "expert", ("dp", "tensor")),
        P(None, "expert", ("dp", "tensor")),
    )
    out_specs = P(None, ("groups", "expert", "dp"), "tensor")
    return jax.shard_map(local, mesh=mesh, in_specs=in_specs, out_specs=out_specs, check_vma=False)
```

```python
import functools

import jax
import jax.numpy as jnp
from jax import lax
from jax.experimental import pallas as pl
from jax.experimental.pallas import tpu as pltpu
from jax.sharding import PartitionSpec as P

HEAD_DIM = 64


def attend(query_row, key_cache, value_cache, key_new, value_new, lengths, moment):
    batch_size = query_row.shape[0]
    groups = key_cache.shape[2] // HEAD_DIM
    per_group = query_row.shape[1] // (groups * HEAD_DIM)
    window = key_cache.shape[1]
    new_count = key_new.shape[0]
    queries = query_row.reshape(batch_size, groups, per_group, HEAD_DIM)
    old_keys = key_cache.reshape(batch_size, window, groups, HEAD_DIM)
    old_values = value_cache.reshape(batch_size, window, groups, HEAD_DIM)
    new_keys = key_new.reshape(new_count, batch_size, groups, HEAD_DIM)
    new_values = value_new.reshape(new_count, batch_size, groups, HEAD_DIM)
    factor = HEAD_DIM ** (-0.5)
    old_scores = (
        jnp.einsum("bgrd,bcgd->bgrc", queries, old_keys, preferred_element_type=jnp.float32)
        * factor
    )
    new_scores = (
        jnp.einsum("bgrd,sbgd->bgrs", queries, new_keys, preferred_element_type=jnp.float32)
        * factor
    )
    old_valid = (jnp.arange(window)[None, :] < lengths[:, None])[:, None, None, :]
    new_valid = (jnp.arange(new_count) <= moment)[None, None, None, :]
    scores = jnp.concatenate(
        [jnp.where(old_valid, old_scores, -jnp.inf), jnp.where(new_valid, new_scores, -jnp.inf)],
        axis=-1,
    )
    highest = jnp.max(scores, axis=-1, keepdims=True)
    powers = jnp.exp(scores - highest)
    weights = (powers / jnp.sum(powers, axis=-1, keepdims=True)).astype(jnp.bfloat16)
    attended = jnp.einsum(
        "bgrc,bcgd->bgrd", weights[..., :window], old_values, preferred_element_type=jnp.float32
    )
    attended = attended + jnp.einsum(
        "bgrs,sbgd->bgrd", weights[..., window:], new_values, preferred_element_type=jnp.float32
    )
    return attended.reshape(batch_size, groups * per_group * HEAD_DIM).astype(jnp.bfloat16)


def move_weights(
    x_res,
    query_new,
    key_new,
    value_new,
    key_cache,
    value_cache,
    lengths,
    routes,
    route_weight,
    norm_gain,
    out_weight,
    w_gate,
    w_up,
    w_down,
):
    expert_count = lax.axis_size("expert")
    row_count = lax.axis_size("dp")
    half_count = lax.axis_size("tensor")
    total_experts = w_gate.shape[0]
    owned_count = total_experts // expert_count
    copies = row_count // owned_count
    tokens = x_res.shape[1]
    choose_k = routes.shape[2]
    capacity = 2 * max(1, tokens * choose_k // total_experts)
    slot_count = capacity // copies
    width = x_res.shape[2]
    row_part = w_gate.shape[1]
    col_part = w_gate.shape[2]
    sectioned = tuple(
        (
            matrix.reshape(expert_count, owned_count, row_part, col_part)
            for matrix in (w_gate, w_up, w_down)
        )
    )
    doubled = tuple((jnp.repeat(matrix, copies, axis=1) for matrix in sectioned))
    placed = (
        lax.all_to_all(
            lax.all_to_all(doubled[0], "expert", split_axis=0, concat_axis=2, tiled=True),
            "dp",
            split_axis=1,
            concat_axis=3,
            tiled=True,
        ),
        lax.all_to_all(
            lax.all_to_all(doubled[1], "expert", split_axis=0, concat_axis=2, tiled=True),
            "dp",
            split_axis=1,
            concat_axis=3,
            tiled=True,
        ),
        lax.all_to_all(
            lax.all_to_all(doubled[2], "expert", split_axis=0, concat_axis=2, tiled=True),
            "dp",
            split_axis=1,
            concat_axis=3,
            tiled=True,
        ),
    )
    gate_w, up_w, down_w = (matrix.reshape(width, -1) for matrix in placed)
    out_proj = lax.all_gather(out_weight, "dp", axis=1, tiled=True)
    lane_ids = jnp.arange(expert_count * row_count * slot_count, dtype=jnp.int32)
    half_width = width // half_count
    results = []
    for moment in range(query_new.shape[0]):
        attended = attend(
            query_new[moment], key_cache, value_cache, key_new, value_new, lengths, moment
        )
        partial_value = jnp.dot(attended, out_proj, preferred_element_type=jnp.float32)
        hidden_state = x_res[moment].astype(jnp.float32) + lax.psum(partial_value, "tensor")
        mean_square = jnp.mean(hidden_state * hidden_state, axis=-1, keepdims=True)
        normed = (hidden_state * lax.rsqrt(mean_square + 1e-05) * norm_gain).astype(jnp.bfloat16)
        chosen = routes[moment].reshape(-1)
        matches = (chosen[:, None] == jnp.arange(total_experts, dtype=jnp.int32)[None, :]).astype(
            jnp.int32
        )
        before = jnp.cumsum(matches, axis=0) - matches
        order_rank = jnp.sum(before * matches, axis=1)
        target = (
            chosen // owned_count * row_count
            + chosen % owned_count * copies
            + order_rank // slot_count
        )
        lane_of = target * slot_count + order_rank % slot_count
        selector = lane_of[:, None] == lane_ids[None, :]
        per_token = jnp.any(selector.reshape(tokens, choose_k, -1), axis=1)
        outgoing = jnp.dot(
            per_token.T.astype(jnp.bfloat16), normed, preferred_element_type=jnp.float32
        ).astype(jnp.bfloat16)
        arrived = lax.all_to_all(
            outgoing.reshape(expert_count * row_count, slot_count, width),
            ("expert", "dp"),
            split_axis=0,
            concat_axis=0,
            tiled=True,
        )
        slot_rows = arrived.reshape(-1, width)
        gate_act = jnp.dot(slot_rows, gate_w, preferred_element_type=jnp.float32)
        up_act = jnp.dot(slot_rows, up_w, preferred_element_type=jnp.float32)
        activated = (jax.nn.silu(gate_act) * up_act).astype(jnp.bfloat16)
        partial_out = lax.dot_general(
            activated, down_w, (((1,), (1,)), ((), ())), preferred_element_type=jnp.float32
        )
        expert_out = lax.psum(partial_out, "tensor").astype(jnp.bfloat16)
        out_width = expert_out.shape[1]
        returned = lax.all_to_all(
            expert_out.reshape(expert_count * row_count, slot_count, out_width),
            ("expert", "dp"),
            split_axis=0,
            concat_axis=0,
            tiled=True,
        )
        gathered = jnp.dot(
            selector.astype(jnp.bfloat16),
            returned.reshape(-1, out_width),
            preferred_element_type=jnp.float32,
        )
        gathered = gathered.reshape(tokens, choose_k, out_width)
        combined = jnp.sum(route_weight[moment][:, :, None] * gathered, axis=1)
        whole_out = (hidden_state + combined).astype(jnp.bfloat16)
        results.append(
            lax.dynamic_slice_in_dim(
                whole_out, lax.axis_index("tensor") * half_width, half_width, 1
            )
        )
    return jnp.stack(results)


def attend_steps(query_new, key_cache, value_cache, key_new, value_new, lengths):
    steps, batch_size, query_width = query_new.shape
    groups = key_cache.shape[2] // HEAD_DIM
    per_group = query_width // (groups * HEAD_DIM)
    window = key_cache.shape[1]
    queries = query_new.reshape(steps, batch_size, groups, per_group, HEAD_DIM)
    queries = queries.transpose(1, 2, 0, 3, 4).reshape(
        batch_size, groups, steps * per_group, HEAD_DIM
    )
    keys = jnp.concatenate([key_cache, key_new.transpose(1, 0, 2)], axis=1)
    values = jnp.concatenate([value_cache, value_new.transpose(1, 0, 2)], axis=1)
    spots = window + steps
    keys = keys.reshape(batch_size, spots, groups, HEAD_DIM)
    values = values.reshape(batch_size, spots, groups, HEAD_DIM)
    scores = jnp.einsum("bgrd,bcgd->bgrc", queries, keys, preferred_element_type=jnp.float32)
    scores = scores * HEAD_DIM ** (-0.5)
    spot = jnp.arange(spots)[None, None, None, :]
    moment = (jnp.arange(steps * per_group) // per_group)[None, None, :, None]
    limit = lengths[:, None, None, None]
    valid = (spot < limit) | ((spot >= window) & (spot - window <= moment))
    scores = jnp.where(valid, scores, -jnp.inf)
    powers = jnp.exp(scores - jnp.max(scores, axis=-1, keepdims=True))
    probs = (powers / jnp.sum(powers, axis=-1, keepdims=True)).astype(jnp.bfloat16)
    attended = jnp.einsum("bgrc,bcgd->bgrd", probs, values, preferred_element_type=jnp.float32)
    attended = attended.astype(jnp.bfloat16).reshape(
        batch_size, groups, steps, per_group, HEAD_DIM
    )
    return attended.transpose(2, 0, 1, 3, 4).reshape(steps * batch_size, query_width)


def layer_kernel(
    slices,
    rows,
    halves,
    top,
    att_ref,
    packed_ref,
    x_ref,
    gain_ref,
    out_ref_w,
    gate_hbm,
    up_hbm,
    down_hbm,
    result_ref,
    gate_ref,
    up_ref,
    down_ref,
    routing,
    att_other,
    proj_out,
    proj_in,
    hidden,
    norm_out,
    features,
    sums_out,
    sums_in,
    act_all,
    down_out,
    down_in,
    part_out,
    part_in,
    final,
    weight_sem,
    att_sem,
    route_sem,
    proj_sem,
    norm_sem,
    sums_sem,
    act_sem,
    down_sem,
    part_sem,
    swap_sem,
):
    f32, bf16 = jnp.float32, jnp.bfloat16
    z, x, c = lax.axis_index("expert"), lax.axis_index("dp"), lax.axis_index("tensor")
    quad = rows * halves
    count = slices * quad
    here = x * halves + c
    me = z * quad + here
    per = out_ref_w.shape[0]
    block = x_ref.shape[2]
    part = x_ref.shape[3]
    experts = gate_ref.shape[0]

    def device(index):
        return {"expert": index // quad, "dp": (index // halves) % rows, "tensor": index % halves}

    def send(source, target, sems, slot, index):
        return pltpu.make_async_remote_copy(
            src_ref=source,
            dst_ref=target,
            send_sem=sems.at[0, slot],
            recv_sem=sems.at[1, slot],
            device_id=device(index),
            device_id_type=pl.DeviceIdType.MESH,
        )

    loads = [
        pltpu.make_async_copy(source, target, weight_sem.at[i])
        for i, (source, target) in enumerate(
            ((gate_hbm, gate_ref), (up_hbm, up_ref), (down_hbm, down_ref))
        )
    ]
    for load in loads:
        load.start()

    barrier = pltpu.get_barrier_semaphore()
    for d in range(1, count):
        pl.semaphore_signal(
            barrier,
            inc=1,
            device_id=device(lax.rem(me + d, count)),
            device_id_type=pl.DeviceIdType.MESH,
        )
    pl.semaphore_wait(barrier, count - 1)

    att_copies = []
    for d in range(1, rows):
        peer = z * quad + lax.rem(x + d, rows) * halves + c
        att_copies.append(send(att_ref, att_other.at[d - 1], att_sem, d, peer))
        att_copies[-1].start()
    route_copies = []
    for d in range(1, count):
        peer = lax.rem(me + d, count)
        route_copies.append(send(packed_ref.at[c], routing.at[me], route_sem, d, peer))
        route_copies[-1].start()
    routing[me] = packed_ref[c]

    def project(value, owner):
        for j in range(per):
            product = jnp.dot(value, out_ref_w[j], preferred_element_type=f32)
            for h in range(halves):
                proj_out[owner * halves + h, j] = product[h * block : (h + 1) * block]

    project(att_ref[...], x)
    for d in range(1, rows):
        att_copies[d - 1].wait()
        project(att_other[d - 1], lax.rem(x - d + rows, rows))

    proj_copies = []
    for d in range(1, quad):
        spot = lax.rem(here + d, quad)
        proj_copies.append(
            send(proj_out.at[spot], proj_in.at[here], proj_sem, d, z * quad + spot)
        )
        proj_copies[-1].start()
    proj_in[here] = proj_out[here]
    for copy in proj_copies:
        copy.wait()

    square = jnp.zeros((block, 1), f32)
    for q in range(slices):
        value = x_ref[c, q].astype(f32)
        for h in range(halves):
            value = value + proj_in[(q // per) * halves + h, q % per]
        hidden[q] = value
        square = square + jnp.sum(value * value, axis=1, keepdims=True)
    scale = lax.rsqrt(square / (slices * part) + 1e-05)
    for q in range(slices):
        norm_out[q] = (hidden[q] * scale * gain_ref[q]).astype(bf16)

    norm_copies = []
    for d in range(1, count):
        peer = lax.rem(me + d, count)
        norm_copies.append(send(norm_out.at[peer // quad], features.at[me], norm_sem, d, peer))
        norm_copies[-1].start()
    features[me] = norm_out[z]
    for copy in route_copies:
        copy.wait()
    for copy in norm_copies:
        copy.wait()
    for load in loads:
        load.wait()

    def sums_copy(d):
        target = lax.rem(z + d, slices)
        return send(sums_out.at[target], sums_in.at[z], sums_sem, d, target * quad + here)

    def marks(zone):
        table = routing[pl.ds(zone * quad, quad)].reshape(quad * block, routing.shape[2])
        return table

    def up_step(i, carry):
        d = lax.rem(i + 1, slices)
        zone = lax.rem(z + d, slices)
        value = features[pl.ds(zone * quad, quad)].reshape(quad * block, part)
        table = marks(zone)
        for g, matrix in enumerate((gate_ref, up_ref)):
            picked = [jnp.zeros((quad * block, matrix.shape[2]), f32)] * top
            for e in range(experts):
                dense = jnp.dot(value, matrix[e], preferred_element_type=f32)
                for k in range(top):
                    picked[k] = jnp.where(table[:, k : k + 1] == float(e), dense, picked[k])
            for k in range(top):
                sums_out[zone, g * top + k] = picked[k].astype(bf16)

        @pl.when(i < slices - 1)
        def _():
            sums_copy(d).start()

        return carry

    lax.fori_loop(0, slices, up_step, 0)
    sums_in[z] = sums_out[z]
    for d in range(1, slices):
        sums_copy(d).wait()

    table = marks(z)
    for k in range(top):
        gate = jnp.zeros(sums_in.shape[2:], f32)
        up = jnp.zeros(sums_in.shape[2:], f32)
        for q in range(slices):
            gate = gate + sums_in[q, k].astype(f32)
            up = up + sums_in[q, top + k].astype(f32)
        value = gate / (1.0 + jnp.exp(-gate)) * up * table[:, top + k : top + k + 1]
        act_all[z, k] = value.astype(bf16)

    def act_copy(d):
        target = lax.rem(z + d, slices)
        return send(act_all.at[z], act_all.at[z], act_sem, d, target * quad + here)

    for d in range(1, slices):
        act_copy(d).start()

    def down_copy(zone, d):
        spot = lax.rem(here + d, quad)
        return pltpu.make_async_remote_copy(
            src_ref=down_out.at[zone, spot],
            dst_ref=down_in.at[zone, here],
            send_sem=down_sem.at[0, zone, d],
            recv_sem=down_sem.at[1, zone, d],
            device_id=device(z * quad + spot),
            device_id_type=pl.DeviceIdType.MESH,
        )

    def down_step(i, carry):
        zone = lax.rem(z - i + slices, slices)

        @pl.when(i > 0)
        def _():
            act_copy(i).wait()

        table = marks(zone)
        total = jnp.zeros((quad * block, part), f32)
        for e in range(experts):
            spread = jnp.zeros(act_all.shape[2:], bf16)
            for k in range(top):
                spread = jnp.where(table[:, k : k + 1] == float(e), act_all[zone, k], spread)
            total = total + lax.dot_general(
                spread, down_ref[e], (((1,), (1,)), ((), ())), preferred_element_type=f32
            )
        down_out[zone] = total.reshape(quad, block, part)
        for d in range(1, quad):
            down_copy(zone, d).start()
        return carry

    lax.fori_loop(0, slices, down_step, 0)

    def part_copy(d):
        target = lax.rem(z + d, slices)
        return send(part_out.at[target], part_in.at[z], part_sem, d, target * quad + here)

    for i in range(slices):
        zone = lax.rem(z - i + slices, slices)
        down_in[zone, here] = down_out[zone, here]
        for d in range(1, quad):
            down_copy(zone, d).wait()
        value = down_in[zone, 0]
        for s in range(1, quad):
            value = value + down_in[zone, s]
        part_out[zone] = value
        if i > 0:
            part_copy((slices - i) % slices).start()
    part_in[z] = part_out[z]
    for d in range(1, slices):
        part_copy(d).wait()
    for q in range(slices):
        final[q] = (hidden[q] + part_in[q]).astype(bf16)

    share = slices // halves
    swaps = []
    for d in range(1, halves):
        other = lax.rem(c + d, halves)
        swaps.append(
            send(
                final.at[pl.ds(other * share, share)],
                result_ref.at[c],
                swap_sem,
                d,
                z * quad + x * halves + other,
            )
        )
        swaps[-1].start()
    result_ref[c] = final[pl.ds(c * share, share)]
    for copy in swaps:
        copy.wait()


def move_tokens(
    x_res,
    query_new,
    key_new,
    value_new,
    key_cache,
    value_cache,
    lengths,
    routes,
    route_weight,
    norm_gain,
    out_weight,
    w_gate,
    w_up,
    w_down,
):
    slices = lax.axis_size("expert")
    rows = lax.axis_size("dp")
    halves = lax.axis_size("tensor")
    experts, part, hidden_part = w_gate.shape
    steps, tokens, width = x_res.shape
    top = routes.shape[2]
    mine = steps * tokens
    block = mine // halves
    quad = rows * halves
    count = slices * quad
    share = slices // halves
    f32, bf16 = jnp.float32, jnp.bfloat16

    packed = jnp.concatenate([routes.astype(f32), route_weight], axis=2)
    packed = packed.reshape(halves, block, 2 * top)
    packed = jnp.pad(packed, ((0, 0), (0, 0), (0, 128 - 2 * top)))
    attended = attend_steps(query_new, key_cache, value_cache, key_new, value_new, lengths)
    residual = x_res.reshape(halves, block, slices, part).transpose(0, 2, 1, 3)
    gain = norm_gain.reshape(slices, 1, part)
    per = out_weight.shape[1] // part
    projection = out_weight.reshape(out_weight.shape[0], per, part).transpose(1, 0, 2)
    vmem = pl.BlockSpec(memory_space=pltpu.VMEM)
    anywhere = pl.BlockSpec(memory_space=pl.ANY)
    dma = pltpu.SemaphoreType.DMA
    result = pl.pallas_call(
        functools.partial(layer_kernel, slices, rows, halves, top),
        out_shape=jax.ShapeDtypeStruct((halves, share, block, part), bf16),
        in_specs=[vmem] * 5 + [anywhere] * 3,
        out_specs=vmem,
        scratch_shapes=[
            pltpu.VMEM(w_gate.shape, bf16),
            pltpu.VMEM(w_up.shape, bf16),
            pltpu.VMEM(w_down.shape, bf16),
            pltpu.VMEM((count, block, 128), f32),
            pltpu.VMEM((rows - 1,) + attended.shape, bf16),
            pltpu.VMEM((quad, per, block, part), f32),
            pltpu.VMEM((quad, per, block, part), f32),
            pltpu.VMEM((slices, block, part), f32),
            pltpu.VMEM((slices, block, part), bf16),
            pltpu.VMEM((count, block, part), bf16),
            pltpu.VMEM((slices, 2 * top, quad * block, hidden_part), bf16),
            pltpu.VMEM((slices, 2 * top, quad * block, hidden_part), bf16),
            pltpu.VMEM((slices, top, quad * block, hidden_part), bf16),
            pltpu.VMEM((slices, quad, block, part), f32),
            pltpu.VMEM((slices, quad, block, part), f32),
            pltpu.VMEM((slices, block, part), f32),
            pltpu.VMEM((slices, block, part), f32),
            pltpu.VMEM((slices, block, part), bf16),
            dma((3,)),
            dma((2, rows)),
            dma((2, count)),
            dma((2, quad)),
            dma((2, count)),
            dma((2, slices)),
            dma((2, slices)),
            dma((2, slices, quad)),
            dma((2, slices)),
            dma((2, halves)),
        ],
        compiler_params=pltpu.CompilerParams(
            collective_id=0, has_side_effects=True, vmem_limit_bytes=40 * 1024 * 1024
        ),
    )(attended, packed, residual, gain, projection, w_gate, w_up, w_down)
    result = result.transpose(0, 2, 1, 3)
    return result.reshape(steps, tokens, width // halves)


def local(*args):
    x_res, routes, w_gate = args[0], args[7], args[11]
    spread = lax.axis_size("expert") * lax.axis_size("dp")
    travelling = x_res.shape[0] * x_res.shape[1] * spread * routes.shape[2]
    if travelling < w_gate.shape[0] * w_gate.shape[1]:
        return move_tokens(*args)
    return move_weights(*args)


def solution(mesh):
    in_specs = (
        P(None, ("groups", "expert", "dp"), None),
        P(None, ("groups", "expert", "dp"), "tensor"),
        P(None, ("groups", "expert", "dp"), "tensor"),
        P(None, ("groups", "expert", "dp"), "tensor"),
        P(("groups", "expert", "dp"), None, "tensor"),
        P(("groups", "expert", "dp"), None, "tensor"),
        P(("groups", "expert", "dp")),
        P(None, ("groups", "expert", "dp"), None),
        P(None, ("groups", "expert", "dp"), None),
        P(),
        P("tensor", "dp"),
        P(None, "expert", ("dp", "tensor")),
        P(None, "expert", ("dp", "tensor")),
        P(None, "expert", ("dp", "tensor")),
    )
    out_specs = P(None, ("groups", "expert", "dp"), "tensor")
    return jax.shard_map(local, mesh=mesh, in_specs=in_specs, out_specs=out_specs, check_vma=False)
```

```python
import functools

import jax
import jax.numpy as jnp
from jax import lax
from jax.experimental import pallas as pl
from jax.experimental.pallas import tpu as pltpu
from jax.sharding import PartitionSpec as P

HEAD_DIM = 64


def attend(query_row, key_cache, value_cache, key_new, value_new, lengths, moment):
    batch_size = query_row.shape[0]
    groups = key_cache.shape[2] // HEAD_DIM
    per_group = query_row.shape[1] // (groups * HEAD_DIM)
    window = key_cache.shape[1]
    new_count = key_new.shape[0]
    queries = query_row.reshape(batch_size, groups, per_group, HEAD_DIM)
    old_keys = key_cache.reshape(batch_size, window, groups, HEAD_DIM)
    old_values = value_cache.reshape(batch_size, window, groups, HEAD_DIM)
    new_keys = key_new.reshape(new_count, batch_size, groups, HEAD_DIM)
    new_values = value_new.reshape(new_count, batch_size, groups, HEAD_DIM)
    factor = HEAD_DIM ** (-0.5)
    old_scores = (
        jnp.einsum("bgrd,bcgd->bgrc", queries, old_keys, preferred_element_type=jnp.float32)
        * factor
    )
    new_scores = (
        jnp.einsum("bgrd,sbgd->bgrs", queries, new_keys, preferred_element_type=jnp.float32)
        * factor
    )
    old_valid = (jnp.arange(window)[None, :] < lengths[:, None])[:, None, None, :]
    new_valid = (jnp.arange(new_count) <= moment)[None, None, None, :]
    scores = jnp.concatenate(
        [jnp.where(old_valid, old_scores, -jnp.inf), jnp.where(new_valid, new_scores, -jnp.inf)],
        axis=-1,
    )
    highest = jnp.max(scores, axis=-1, keepdims=True)
    powers = jnp.exp(scores - highest)
    weights = (powers / jnp.sum(powers, axis=-1, keepdims=True)).astype(jnp.bfloat16)
    attended = jnp.einsum(
        "bgrc,bcgd->bgrd", weights[..., :window], old_values, preferred_element_type=jnp.float32
    )
    attended = attended + jnp.einsum(
        "bgrs,sbgd->bgrd", weights[..., window:], new_values, preferred_element_type=jnp.float32
    )
    return attended.reshape(batch_size, groups * per_group * HEAD_DIM).astype(jnp.bfloat16)


def move_weights(
    x_res,
    query_new,
    key_new,
    value_new,
    key_cache,
    value_cache,
    lengths,
    routes,
    route_weight,
    norm_gain,
    out_weight,
    w_gate,
    w_up,
    w_down,
):
    expert_count = lax.axis_size("expert")
    row_count = lax.axis_size("dp")
    half_count = lax.axis_size("tensor")
    total_experts = w_gate.shape[0]
    owned_count = total_experts // expert_count
    copies = row_count // owned_count
    tokens = x_res.shape[1]
    choose_k = routes.shape[2]
    capacity = 2 * max(1, tokens * choose_k // total_experts)
    slot_count = capacity // copies
    width = x_res.shape[2]
    row_part = w_gate.shape[1]
    col_part = w_gate.shape[2]
    sectioned = tuple(
        (
            matrix.reshape(expert_count, owned_count, row_part, col_part)
            for matrix in (w_gate, w_up, w_down)
        )
    )
    doubled = tuple((jnp.repeat(matrix, copies, axis=1) for matrix in sectioned))
    placed = (
        lax.all_to_all(
            lax.all_to_all(doubled[0], "expert", split_axis=0, concat_axis=2, tiled=True),
            "dp",
            split_axis=1,
            concat_axis=3,
            tiled=True,
        ),
        lax.all_to_all(
            lax.all_to_all(doubled[1], "expert", split_axis=0, concat_axis=2, tiled=True),
            "dp",
            split_axis=1,
            concat_axis=3,
            tiled=True,
        ),
        lax.all_to_all(
            lax.all_to_all(doubled[2], "expert", split_axis=0, concat_axis=2, tiled=True),
            "dp",
            split_axis=1,
            concat_axis=3,
            tiled=True,
        ),
    )
    gate_w, up_w, down_w = (matrix.reshape(width, -1) for matrix in placed)
    out_proj = lax.all_gather(out_weight, "dp", axis=1, tiled=True)
    lane_ids = jnp.arange(expert_count * row_count * slot_count, dtype=jnp.int32)
    half_width = width // half_count
    results = []
    for moment in range(query_new.shape[0]):
        attended = attend(
            query_new[moment], key_cache, value_cache, key_new, value_new, lengths, moment
        )
        partial_value = jnp.dot(attended, out_proj, preferred_element_type=jnp.float32)
        hidden_state = x_res[moment].astype(jnp.float32) + lax.psum(partial_value, "tensor")
        mean_square = jnp.mean(hidden_state * hidden_state, axis=-1, keepdims=True)
        normed = (hidden_state * lax.rsqrt(mean_square + 1e-05) * norm_gain).astype(jnp.bfloat16)
        chosen = routes[moment].reshape(-1)
        matches = (chosen[:, None] == jnp.arange(total_experts, dtype=jnp.int32)[None, :]).astype(
            jnp.int32
        )
        before = jnp.cumsum(matches, axis=0) - matches
        order_rank = jnp.sum(before * matches, axis=1)
        target = (
            chosen // owned_count * row_count
            + chosen % owned_count * copies
            + order_rank // slot_count
        )
        lane_of = target * slot_count + order_rank % slot_count
        selector = lane_of[:, None] == lane_ids[None, :]
        per_token = jnp.any(selector.reshape(tokens, choose_k, -1), axis=1)
        outgoing = jnp.dot(
            per_token.T.astype(jnp.bfloat16), normed, preferred_element_type=jnp.float32
        ).astype(jnp.bfloat16)
        arrived = lax.all_to_all(
            outgoing.reshape(expert_count * row_count, slot_count, width),
            ("expert", "dp"),
            split_axis=0,
            concat_axis=0,
            tiled=True,
        )
        slot_rows = arrived.reshape(-1, width)
        gate_act = jnp.dot(slot_rows, gate_w, preferred_element_type=jnp.float32)
        up_act = jnp.dot(slot_rows, up_w, preferred_element_type=jnp.float32)
        activated = (jax.nn.silu(gate_act) * up_act).astype(jnp.bfloat16)
        partial_out = lax.dot_general(
            activated, down_w, (((1,), (1,)), ((), ())), preferred_element_type=jnp.float32
        )
        expert_out = lax.psum(partial_out, "tensor").astype(jnp.bfloat16)
        out_width = expert_out.shape[1]
        returned = lax.all_to_all(
            expert_out.reshape(expert_count * row_count, slot_count, out_width),
            ("expert", "dp"),
            split_axis=0,
            concat_axis=0,
            tiled=True,
        )
        gathered = jnp.dot(
            selector.astype(jnp.bfloat16),
            returned.reshape(-1, out_width),
            preferred_element_type=jnp.float32,
        )
        gathered = gathered.reshape(tokens, choose_k, out_width)
        combined = jnp.sum(route_weight[moment][:, :, None] * gathered, axis=1)
        whole_out = (hidden_state + combined).astype(jnp.bfloat16)
        results.append(
            lax.dynamic_slice_in_dim(
                whole_out, lax.axis_index("tensor") * half_width, half_width, 1
            )
        )
    return jnp.stack(results)


def attend_steps(query_new, key_cache, value_cache, key_new, value_new, lengths):
    steps, batch_size, query_width = query_new.shape
    groups = key_cache.shape[2] // HEAD_DIM
    per_group = query_width // (groups * HEAD_DIM)
    window = key_cache.shape[1]
    queries = query_new.reshape(steps, batch_size, groups, per_group, HEAD_DIM)
    queries = queries.transpose(1, 2, 0, 3, 4).reshape(
        batch_size, groups, steps * per_group, HEAD_DIM
    )
    keys = jnp.concatenate([key_cache, key_new.transpose(1, 0, 2)], axis=1)
    values = jnp.concatenate([value_cache, value_new.transpose(1, 0, 2)], axis=1)
    spots = window + steps
    keys = keys.reshape(batch_size, spots, groups, HEAD_DIM)
    values = values.reshape(batch_size, spots, groups, HEAD_DIM)
    scores = jnp.einsum("bgrd,bcgd->bgrc", queries, keys, preferred_element_type=jnp.float32)
    scores = scores * HEAD_DIM ** (-0.5)
    spot = jnp.arange(spots)[None, None, None, :]
    moment = (jnp.arange(steps * per_group) // per_group)[None, None, :, None]
    limit = lengths[:, None, None, None]
    valid = (spot < limit) | ((spot >= window) & (spot - window <= moment))
    scores = jnp.where(valid, scores, -jnp.inf)
    powers = jnp.exp(scores - jnp.max(scores, axis=-1, keepdims=True))
    probs = (powers / jnp.sum(powers, axis=-1, keepdims=True)).astype(jnp.bfloat16)
    attended = jnp.einsum("bgrc,bcgd->bgrd", probs, values, preferred_element_type=jnp.float32)
    attended = attended.astype(jnp.bfloat16).reshape(
        batch_size, groups, steps, per_group, HEAD_DIM
    )
    return attended.transpose(2, 0, 1, 3, 4).reshape(steps * batch_size, query_width)


def layer_kernel(
    slices,
    rows,
    halves,
    top,
    att_ref,
    packed_ref,
    x_ref,
    gain_ref,
    out_ref_w,
    gate_hbm,
    up_hbm,
    down_hbm,
    result_ref,
    gate_ref,
    up_ref,
    down_ref,
    routing,
    att_other,
    proj_out,
    proj_in,
    hidden,
    norm_out,
    features,
    partial,
    sums_out,
    sums_in,
    act_all,
    down_out,
    down_in,
    part_out,
    part_in,
    final,
    weight_sem,
    att_sem,
    route_sem,
    proj_sem,
    norm_sem,
    sums_sem,
    act_sem,
    down_sem,
    part_sem,
    swap_sem,
):
    f32, bf16 = jnp.float32, jnp.bfloat16
    z, x, c = lax.axis_index("expert"), lax.axis_index("dp"), lax.axis_index("tensor")
    quad = rows * halves
    count = slices * quad
    here = x * halves + c
    me = z * quad + here
    per = out_ref_w.shape[0]
    block = x_ref.shape[2]
    part = x_ref.shape[3]
    experts = gate_ref.shape[0]

    def device(index):
        return {"expert": index // quad, "dp": (index // halves) % rows, "tensor": index % halves}

    def send(source, target, sems, slot, index):
        return pltpu.make_async_remote_copy(
            src_ref=source,
            dst_ref=target,
            send_sem=sems.at[0, slot],
            recv_sem=sems.at[1, slot],
            device_id=device(index),
            device_id_type=pl.DeviceIdType.MESH,
        )

    loads = [
        pltpu.make_async_copy(source, target, weight_sem.at[i])
        for i, (source, target) in enumerate(
            ((gate_hbm, gate_ref), (up_hbm, up_ref), (down_hbm, down_ref))
        )
    ]
    for load in loads:
        load.start()

    barrier = pltpu.get_barrier_semaphore()
    for d in range(1, count):
        pl.semaphore_signal(
            barrier,
            inc=1,
            device_id=device(lax.rem(me + d, count)),
            device_id_type=pl.DeviceIdType.MESH,
        )
    pl.semaphore_wait(barrier, count - 1)

    att_copies = []
    for d in range(1, rows):
        peer = z * quad + lax.rem(x + d, rows) * halves + c
        att_copies.append(send(att_ref, att_other.at[d - 1], att_sem, d, peer))
        att_copies[-1].start()
    route_copies = []
    for d in range(1, count):
        peer = lax.rem(me + d, count)
        route_copies.append(send(packed_ref.at[c], routing.at[me], route_sem, d, peer))
        route_copies[-1].start()
    routing[me] = packed_ref[c]

    def project(value, owner):
        for j in range(per):
            product = jnp.dot(value, out_ref_w[j], preferred_element_type=f32)
            for h in range(halves):
                proj_out[owner * halves + h, j] = product[h * block : (h + 1) * block]

    project(att_ref[...], x)
    for d in range(1, rows):
        att_copies[d - 1].wait()
        project(att_other[d - 1], lax.rem(x - d + rows, rows))

    proj_copies = []
    for d in range(1, quad):
        spot = lax.rem(here + d, quad)
        proj_copies.append(
            send(proj_out.at[spot], proj_in.at[here], proj_sem, d, z * quad + spot)
        )
        proj_copies[-1].start()
    proj_in[here] = proj_out[here]
    for copy in proj_copies:
        copy.wait()

    square = jnp.zeros((block, 1), f32)
    for q in range(slices):
        value = x_ref[c, q].astype(f32)
        for h in range(halves):
            value = value + proj_in[(q // per) * halves + h, q % per]
        hidden[q] = value
        square = square + jnp.sum(value * value, axis=1, keepdims=True)
    scale = lax.rsqrt(square / (slices * part) + 1e-05)
    for q in range(slices):
        norm_out[q] = (hidden[q] * scale * gain_ref[q]).astype(bf16)

    norm_copies = []
    for d in range(1, count):
        peer = lax.rem(me + d, count)
        norm_copies.append(send(norm_out.at[peer // quad], features.at[me], norm_sem, d, peer))
        norm_copies[-1].start()
    features[me] = norm_out[z]
    for copy in route_copies:
        copy.wait()
    for copy in norm_copies:
        copy.wait()
    for load in loads:
        load.wait()

    near = slices // 2

    def neighbour(step):
        return lax.rem(z + step + slices, slices) * quad + here

    def sums_copy(zone, g):
        span = pl.ds(g * top, top)
        return pltpu.make_async_remote_copy(
            src_ref=sums_out.at[zone, span],
            dst_ref=sums_in.at[zone, span],
            send_sem=sums_sem.at[0, zone, g],
            recv_sem=sums_sem.at[1, zone, g],
            device_id=device(neighbour(2 * (zone // near) - 1)),
            device_id_type=pl.DeviceIdType.MESH,
        )

    def act_copy(zone):
        return send(
            act_all.at[zone], act_all.at[zone], act_sem, zone, neighbour(1 - 2 * (zone // near))
        )

    def owner(zone):
        return (zone // near) * (slices - 1)

    def source(zone):
        return slices - 1 - owner(zone)

    def marks(zone):
        return routing[pl.ds(zone * quad, quad)].reshape(quad * block, routing.shape[2])

    def relay(zone):
        @pl.when((z != owner(zone)) & (z != source(zone)))
        def _():
            for g in range(2):
                sums_copy(zone, g).wait_recv()
                for k in range(g * top, (g + 1) * top):
                    sums_out[zone, k] = (partial[zone, k] + sums_in[zone, k].astype(f32)).astype(
                        bf16
                    )
                sums_copy(zone, g).start()

    def far_zone(i):
        return lax.rem(i + (1 - z // near) * near, slices)

    def near_zone(i):
        return lax.rem(i + (z // near) * near, slices)

    def up_step(i, carry):
        zone = far_zone(i)
        value = features[pl.ds(zone * quad, quad)].reshape(quad * block, part)
        table = marks(zone)
        for g, matrix in enumerate((gate_ref, up_ref)):
            picked = [jnp.zeros((quad * block, matrix.shape[2]), f32)] * top
            for e in range(experts):
                dense = jnp.dot(value, matrix[e], preferred_element_type=f32)
                for k in range(top):
                    picked[k] = jnp.where(table[:, k : k + 1] == float(e), dense, picked[k])
            for k in range(top):
                partial[zone, g * top + k] = picked[k]

            @pl.when(z == source(zone))
            def _():
                for k in range(g * top, (g + 1) * top):
                    sums_out[zone, k] = partial[zone, k].astype(bf16)
                sums_copy(zone, g).start()

        @pl.when(i > 0)
        def _():
            relay(far_zone(i + slices - 1))

        return carry

    lax.fori_loop(0, slices, up_step, 0)
    relay(far_zone(slices - 1))

    def down_copy(zone, d):
        spot = lax.rem(here + d, quad)
        return pltpu.make_async_remote_copy(
            src_ref=down_out.at[zone, spot],
            dst_ref=down_in.at[zone, here],
            send_sem=down_sem.at[0, zone, d],
            recv_sem=down_sem.at[1, zone, d],
            device_id=device(z * quad + spot),
            device_id_type=pl.DeviceIdType.MESH,
        )

    def down_step(i, carry):
        zone = near_zone(i)

        @pl.when(z == owner(zone))
        def _():
            table = marks(zone)
            for g in range(2):
                sums_copy(zone, g).wait_recv()
            for k in range(top):
                gate = partial[zone, k] + sums_in[zone, k].astype(f32)
                up = partial[zone, top + k] + sums_in[zone, top + k].astype(f32)
                value = gate / (1.0 + jnp.exp(-gate)) * up * table[:, top + k : top + k + 1]
                act_all[zone, k] = value.astype(bf16)

        @pl.when(z != owner(zone))
        def _():
            act_copy(zone).wait_recv()

        @pl.when(z != source(zone))
        def _():
            act_copy(zone).start()

        table = marks(zone)
        total = jnp.zeros((quad * block, part), f32)
        for e in range(experts):
            spread = jnp.zeros(act_all.shape[2:], bf16)
            for k in range(top):
                spread = jnp.where(table[:, k : k + 1] == float(e), act_all[zone, k], spread)
            total = total + lax.dot_general(
                spread, down_ref[e], (((1,), (1,)), ((), ())), preferred_element_type=f32
            )
        down_out[zone] = total.reshape(quad, block, part)
        for d in range(1, quad):
            down_copy(zone, d).start()
        return carry

    lax.fori_loop(0, slices, down_step, 0)

    def settle(zone, carry):
        @pl.when(z != owner(zone))
        def _():
            for g in range(2):
                sums_copy(zone, g).wait_send()

        @pl.when(z != source(zone))
        def _():
            act_copy(zone).wait_send()

        return carry

    lax.fori_loop(0, slices, settle, 0)

    def part_copy(d):
        target = lax.rem(z + d, slices)
        return send(part_out.at[target], part_in.at[z], part_sem, d, target * quad + here)

    for i in range(slices):
        zone = lax.rem(z - i + slices, slices)
        down_in[zone, here] = down_out[zone, here]
        for d in range(1, quad):
            down_copy(zone, d).wait()
        value = down_in[zone, 0]
        for s in range(1, quad):
            value = value + down_in[zone, s]
        part_out[zone] = value
        if i > 0:
            part_copy((slices - i) % slices).start()
    part_in[z] = part_out[z]
    for d in range(1, slices):
        part_copy(d).wait()
    for q in range(slices):
        final[q] = (hidden[q] + part_in[q]).astype(bf16)

    share = slices // halves
    swaps = []
    for d in range(1, halves):
        other = lax.rem(c + d, halves)
        swaps.append(
            send(
                final.at[pl.ds(other * share, share)],
                result_ref.at[c],
                swap_sem,
                d,
                z * quad + x * halves + other,
            )
        )
        swaps[-1].start()
    result_ref[c] = final[pl.ds(c * share, share)]
    for copy in swaps:
        copy.wait()


def move_tokens(
    x_res,
    query_new,
    key_new,
    value_new,
    key_cache,
    value_cache,
    lengths,
    routes,
    route_weight,
    norm_gain,
    out_weight,
    w_gate,
    w_up,
    w_down,
):
    slices = lax.axis_size("expert")
    rows = lax.axis_size("dp")
    halves = lax.axis_size("tensor")
    experts, part, hidden_part = w_gate.shape
    steps, tokens, width = x_res.shape
    top = routes.shape[2]
    mine = steps * tokens
    block = mine // halves
    quad = rows * halves
    count = slices * quad
    share = slices // halves
    f32, bf16 = jnp.float32, jnp.bfloat16

    packed = jnp.concatenate([routes.astype(f32), route_weight], axis=2)
    packed = packed.reshape(halves, block, 2 * top)
    packed = jnp.pad(packed, ((0, 0), (0, 0), (0, 128 - 2 * top)))
    attended = attend_steps(query_new, key_cache, value_cache, key_new, value_new, lengths)
    residual = x_res.reshape(halves, block, slices, part).transpose(0, 2, 1, 3)
    gain = norm_gain.reshape(slices, 1, part)
    per = out_weight.shape[1] // part
    projection = out_weight.reshape(out_weight.shape[0], per, part).transpose(1, 0, 2)
    vmem = pl.BlockSpec(memory_space=pltpu.VMEM)
    anywhere = pl.BlockSpec(memory_space=pl.ANY)
    dma = pltpu.SemaphoreType.DMA
    result = pl.pallas_call(
        functools.partial(layer_kernel, slices, rows, halves, top),
        out_shape=jax.ShapeDtypeStruct((halves, share, block, part), bf16),
        in_specs=[vmem] * 5 + [anywhere] * 3,
        out_specs=vmem,
        scratch_shapes=[
            pltpu.VMEM(w_gate.shape, bf16),
            pltpu.VMEM(w_up.shape, bf16),
            pltpu.VMEM(w_down.shape, bf16),
            pltpu.VMEM((count, block, 128), f32),
            pltpu.VMEM((rows - 1,) + attended.shape, bf16),
            pltpu.VMEM((quad, per, block, part), f32),
            pltpu.VMEM((quad, per, block, part), f32),
            pltpu.VMEM((slices, block, part), f32),
            pltpu.VMEM((slices, block, part), bf16),
            pltpu.VMEM((count, block, part), bf16),
            pltpu.VMEM((slices, 2 * top, quad * block, hidden_part), f32),
            pltpu.VMEM((slices, 2 * top, quad * block, hidden_part), bf16),
            pltpu.VMEM((slices, 2 * top, quad * block, hidden_part), bf16),
            pltpu.VMEM((slices, top, quad * block, hidden_part), bf16),
            pltpu.VMEM((slices, quad, block, part), f32),
            pltpu.VMEM((slices, quad, block, part), f32),
            pltpu.VMEM((slices, block, part), f32),
            pltpu.VMEM((slices, block, part), f32),
            pltpu.VMEM((slices, block, part), bf16),
            dma((3,)),
            dma((2, rows)),
            dma((2, count)),
            dma((2, quad)),
            dma((2, count)),
            dma((2, slices, 2)),
            dma((2, slices)),
            dma((2, slices, quad)),
            dma((2, slices)),
            dma((2, halves)),
        ],
        compiler_params=pltpu.CompilerParams(
            collective_id=0, has_side_effects=True, vmem_limit_bytes=60 * 1024 * 1024
        ),
    )(attended, packed, residual, gain, projection, w_gate, w_up, w_down)
    result = result.transpose(0, 2, 1, 3)
    return result.reshape(steps, tokens, width // halves)


def local(*args):
    x_res, routes, w_gate = args[0], args[7], args[11]
    spread = lax.axis_size("expert") * lax.axis_size("dp")
    travelling = x_res.shape[0] * x_res.shape[1] * spread * routes.shape[2]
    even = lax.axis_size("expert") % 2 == 0
    if even and travelling < w_gate.shape[0] * w_gate.shape[1]:
        return move_tokens(*args)
    return move_weights(*args)


def solution(mesh):
    in_specs = (
        P(None, ("groups", "expert", "dp"), None),
        P(None, ("groups", "expert", "dp"), "tensor"),
        P(None, ("groups", "expert", "dp"), "tensor"),
        P(None, ("groups", "expert", "dp"), "tensor"),
        P(("groups", "expert", "dp"), None, "tensor"),
        P(("groups", "expert", "dp"), None, "tensor"),
        P(("groups", "expert", "dp")),
        P(None, ("groups", "expert", "dp"), None),
        P(None, ("groups", "expert", "dp"), None),
        P(),
        P("tensor", "dp"),
        P(None, "expert", ("dp", "tensor")),
        P(None, "expert", ("dp", "tensor")),
        P(None, "expert", ("dp", "tensor")),
    )
    out_specs = P(None, ("groups", "expert", "dp"), "tensor")
    return jax.shard_map(local, mesh=mesh, in_specs=in_specs, out_specs=out_specs, check_vma=False)
```

```python
import functools

import jax
import jax.numpy as jnp
from jax import lax
from jax.experimental import pallas as pl
from jax.experimental.pallas import tpu as pltpu
from jax.sharding import PartitionSpec as P

HEAD_DIM = 64


def attend(query_row, key_cache, value_cache, key_new, value_new, lengths, moment):
    batch_size = query_row.shape[0]
    groups = key_cache.shape[2] // HEAD_DIM
    per_group = query_row.shape[1] // (groups * HEAD_DIM)
    window = key_cache.shape[1]
    new_count = key_new.shape[0]
    queries = query_row.reshape(batch_size, groups, per_group, HEAD_DIM)
    old_keys = key_cache.reshape(batch_size, window, groups, HEAD_DIM)
    old_values = value_cache.reshape(batch_size, window, groups, HEAD_DIM)
    new_keys = key_new.reshape(new_count, batch_size, groups, HEAD_DIM)
    new_values = value_new.reshape(new_count, batch_size, groups, HEAD_DIM)
    factor = HEAD_DIM ** (-0.5)
    old_scores = (
        jnp.einsum("bgrd,bcgd->bgrc", queries, old_keys, preferred_element_type=jnp.float32)
        * factor
    )
    new_scores = (
        jnp.einsum("bgrd,sbgd->bgrs", queries, new_keys, preferred_element_type=jnp.float32)
        * factor
    )
    old_valid = (jnp.arange(window)[None, :] < lengths[:, None])[:, None, None, :]
    new_valid = (jnp.arange(new_count) <= moment)[None, None, None, :]
    scores = jnp.concatenate(
        [jnp.where(old_valid, old_scores, -jnp.inf), jnp.where(new_valid, new_scores, -jnp.inf)],
        axis=-1,
    )
    highest = jnp.max(scores, axis=-1, keepdims=True)
    powers = jnp.exp(scores - highest)
    weights = (powers / jnp.sum(powers, axis=-1, keepdims=True)).astype(jnp.bfloat16)
    attended = jnp.einsum(
        "bgrc,bcgd->bgrd", weights[..., :window], old_values, preferred_element_type=jnp.float32
    )
    attended = attended + jnp.einsum(
        "bgrs,sbgd->bgrd", weights[..., window:], new_values, preferred_element_type=jnp.float32
    )
    return attended.reshape(batch_size, groups * per_group * HEAD_DIM).astype(jnp.bfloat16)


def move_weights(
    x_res,
    query_new,
    key_new,
    value_new,
    key_cache,
    value_cache,
    lengths,
    routes,
    route_weight,
    norm_gain,
    out_weight,
    w_gate,
    w_up,
    w_down,
):
    expert_count = lax.axis_size("expert")
    row_count = lax.axis_size("dp")
    half_count = lax.axis_size("tensor")
    total_experts = w_gate.shape[0]
    owned_count = total_experts // expert_count
    copies = row_count // owned_count
    tokens = x_res.shape[1]
    choose_k = routes.shape[2]
    capacity = 2 * max(1, tokens * choose_k // total_experts)
    slot_count = capacity // copies
    width = x_res.shape[2]
    row_part = w_gate.shape[1]
    col_part = w_gate.shape[2]
    sectioned = tuple(
        (
            matrix.reshape(expert_count, owned_count, row_part, col_part)
            for matrix in (w_gate, w_up, w_down)
        )
    )
    doubled = tuple((jnp.repeat(matrix, copies, axis=1) for matrix in sectioned))
    placed = (
        lax.all_to_all(
            lax.all_to_all(doubled[0], "expert", split_axis=0, concat_axis=2, tiled=True),
            "dp",
            split_axis=1,
            concat_axis=3,
            tiled=True,
        ),
        lax.all_to_all(
            lax.all_to_all(doubled[1], "expert", split_axis=0, concat_axis=2, tiled=True),
            "dp",
            split_axis=1,
            concat_axis=3,
            tiled=True,
        ),
        lax.all_to_all(
            lax.all_to_all(doubled[2], "expert", split_axis=0, concat_axis=2, tiled=True),
            "dp",
            split_axis=1,
            concat_axis=3,
            tiled=True,
        ),
    )
    gate_w, up_w, down_w = (matrix.reshape(width, -1) for matrix in placed)
    out_proj = lax.all_gather(out_weight, "dp", axis=1, tiled=True)
    lane_ids = jnp.arange(expert_count * row_count * slot_count, dtype=jnp.int32)
    half_width = width // half_count
    results = []
    for moment in range(query_new.shape[0]):
        attended = attend(
            query_new[moment], key_cache, value_cache, key_new, value_new, lengths, moment
        )
        partial_value = jnp.dot(attended, out_proj, preferred_element_type=jnp.float32)
        hidden_state = x_res[moment].astype(jnp.float32) + lax.psum(partial_value, "tensor")
        mean_square = jnp.mean(hidden_state * hidden_state, axis=-1, keepdims=True)
        normed = (hidden_state * lax.rsqrt(mean_square + 1e-05) * norm_gain).astype(jnp.bfloat16)
        chosen = routes[moment].reshape(-1)
        matches = (chosen[:, None] == jnp.arange(total_experts, dtype=jnp.int32)[None, :]).astype(
            jnp.int32
        )
        before = jnp.cumsum(matches, axis=0) - matches
        order_rank = jnp.sum(before * matches, axis=1)
        target = (
            chosen // owned_count * row_count
            + chosen % owned_count * copies
            + order_rank // slot_count
        )
        lane_of = target * slot_count + order_rank % slot_count
        selector = lane_of[:, None] == lane_ids[None, :]
        per_token = jnp.any(selector.reshape(tokens, choose_k, -1), axis=1)
        outgoing = jnp.dot(
            per_token.T.astype(jnp.bfloat16), normed, preferred_element_type=jnp.float32
        ).astype(jnp.bfloat16)
        arrived = lax.all_to_all(
            outgoing.reshape(expert_count * row_count, slot_count, width),
            ("expert", "dp"),
            split_axis=0,
            concat_axis=0,
            tiled=True,
        )
        slot_rows = arrived.reshape(-1, width)
        gate_act = jnp.dot(slot_rows, gate_w, preferred_element_type=jnp.float32)
        up_act = jnp.dot(slot_rows, up_w, preferred_element_type=jnp.float32)
        activated = (jax.nn.silu(gate_act) * up_act).astype(jnp.bfloat16)
        partial_out = lax.dot_general(
            activated, down_w, (((1,), (1,)), ((), ())), preferred_element_type=jnp.float32
        )
        expert_out = lax.psum(partial_out, "tensor").astype(jnp.bfloat16)
        out_width = expert_out.shape[1]
        returned = lax.all_to_all(
            expert_out.reshape(expert_count * row_count, slot_count, out_width),
            ("expert", "dp"),
            split_axis=0,
            concat_axis=0,
            tiled=True,
        )
        gathered = jnp.dot(
            selector.astype(jnp.bfloat16),
            returned.reshape(-1, out_width),
            preferred_element_type=jnp.float32,
        )
        gathered = gathered.reshape(tokens, choose_k, out_width)
        combined = jnp.sum(route_weight[moment][:, :, None] * gathered, axis=1)
        whole_out = (hidden_state + combined).astype(jnp.bfloat16)
        results.append(
            lax.dynamic_slice_in_dim(
                whole_out, lax.axis_index("tensor") * half_width, half_width, 1
            )
        )
    return jnp.stack(results)


def attend_steps(query_new, key_cache, value_cache, key_new, value_new, lengths):
    steps, batch_size, query_width = query_new.shape
    groups = key_cache.shape[2] // HEAD_DIM
    per_group = query_width // (groups * HEAD_DIM)
    window = key_cache.shape[1]
    queries = query_new.reshape(steps, batch_size, groups, per_group, HEAD_DIM)
    queries = queries.transpose(1, 2, 0, 3, 4).reshape(
        batch_size, groups, steps * per_group, HEAD_DIM
    )
    keys = jnp.concatenate([key_cache, key_new.transpose(1, 0, 2)], axis=1)
    values = jnp.concatenate([value_cache, value_new.transpose(1, 0, 2)], axis=1)
    spots = window + steps
    keys = keys.reshape(batch_size, spots, groups, HEAD_DIM)
    values = values.reshape(batch_size, spots, groups, HEAD_DIM)
    scores = jnp.einsum("bgrd,bcgd->bgrc", queries, keys, preferred_element_type=jnp.float32)
    scores = scores * HEAD_DIM ** (-0.5)
    spot = jnp.arange(spots)[None, None, None, :]
    moment = (jnp.arange(steps * per_group) // per_group)[None, None, :, None]
    limit = lengths[:, None, None, None]
    valid = (spot < limit) | ((spot >= window) & (spot - window <= moment))
    scores = jnp.where(valid, scores, -jnp.inf)
    powers = jnp.exp(scores - jnp.max(scores, axis=-1, keepdims=True))
    probs = (powers / jnp.sum(powers, axis=-1, keepdims=True)).astype(jnp.bfloat16)
    attended = jnp.einsum("bgrc,bcgd->bgrd", probs, values, preferred_element_type=jnp.float32)
    attended = attended.astype(jnp.bfloat16).reshape(
        batch_size, groups, steps, per_group, HEAD_DIM
    )
    return attended.transpose(2, 0, 1, 3, 4).reshape(steps * batch_size, query_width)


def layer_kernel(
    slices,
    rows,
    halves,
    top,
    att_ref,
    packed_ref,
    x_ref,
    gain_ref,
    out_ref_w,
    gate_hbm,
    up_hbm,
    down_hbm,
    result_ref,
    gate_ref,
    up_ref,
    down_ref,
    routing,
    att_other,
    proj_out,
    proj_in,
    hidden,
    norm_out,
    features,
    partial,
    sums_out,
    sums_in,
    act_all,
    down_out,
    down_in,
    part_out,
    part_in,
    final,
    weight_sem,
    att_sem,
    route_sem,
    proj_sem,
    norm_sem,
    sums_sem,
    act_sem,
    down_sem,
    part_sem,
    swap_sem,
):
    f32, bf16 = jnp.float32, jnp.bfloat16
    z, x, c = lax.axis_index("expert"), lax.axis_index("dp"), lax.axis_index("tensor")
    quad = rows * halves
    count = slices * quad
    here = x * halves + c
    me = z * quad + here
    per = out_ref_w.shape[0]
    block = x_ref.shape[2]
    part = x_ref.shape[3]
    experts = gate_ref.shape[0]

    def device(index):
        return {"expert": index // quad, "dp": (index // halves) % rows, "tensor": index % halves}

    def send(source, target, sems, slot, index):
        return pltpu.make_async_remote_copy(
            src_ref=source,
            dst_ref=target,
            send_sem=sems.at[0, slot],
            recv_sem=sems.at[1, slot],
            device_id=device(index),
            device_id_type=pl.DeviceIdType.MESH,
        )

    loads = [
        pltpu.make_async_copy(source, target, weight_sem.at[i])
        for i, (source, target) in enumerate(
            ((gate_hbm, gate_ref), (up_hbm, up_ref), (down_hbm, down_ref))
        )
    ]
    for load in loads:
        load.start()

    barrier = pltpu.get_barrier_semaphore()
    for d in range(1, count):
        pl.semaphore_signal(
            barrier,
            inc=1,
            device_id=device(lax.rem(me + d, count)),
            device_id_type=pl.DeviceIdType.MESH,
        )
    pl.semaphore_wait(barrier, count - 1)

    att_copies = []
    for d in range(1, rows):
        peer = z * quad + lax.rem(x + d, rows) * halves + c
        att_copies.append(send(att_ref, att_other.at[d - 1], att_sem, d, peer))
        att_copies[-1].start()
    route_copies = []
    for d in range(1, count):
        peer = lax.rem(me + d, count)
        route_copies.append(send(packed_ref.at[c], routing.at[me], route_sem, d, peer))
        route_copies[-1].start()
    routing[me] = packed_ref[c]

    def project(value, owner):
        for j in range(per):
            product = jnp.dot(value, out_ref_w[j], preferred_element_type=f32)
            for h in range(halves):
                proj_out[owner * halves + h, j] = product[h * block : (h + 1) * block]

    project(att_ref[...], x)
    for d in range(1, rows):
        att_copies[d - 1].wait()
        project(att_other[d - 1], lax.rem(x - d + rows, rows))

    proj_copies = []
    for d in range(1, quad):
        spot = lax.rem(here + d, quad)
        proj_copies.append(
            send(proj_out.at[spot], proj_in.at[here], proj_sem, d, z * quad + spot)
        )
        proj_copies[-1].start()
    proj_in[here] = proj_out[here]
    for copy in proj_copies:
        copy.wait()

    square = jnp.zeros((block, 1), f32)
    for q in range(slices):
        value = x_ref[c, q].astype(f32)
        for h in range(halves):
            value = value + proj_in[(q // per) * halves + h, q % per]
        hidden[q] = value
        square = square + jnp.sum(value * value, axis=1, keepdims=True)
    scale = lax.rsqrt(square / (slices * part) + 1e-05)
    for q in range(slices):
        norm_out[q] = (hidden[q] * scale * gain_ref[q]).astype(bf16)

    norm_copies = []
    for d in range(1, count):
        peer = lax.rem(me + d, count)
        norm_copies.append(send(norm_out.at[peer // quad], features.at[me], norm_sem, d, peer))
        norm_copies[-1].start()
    features[me] = norm_out[z]
    for copy in route_copies:
        copy.wait()
    for copy in norm_copies:
        copy.wait()
    for load in loads:
        load.wait()

    near = slices // 2

    def neighbour(step):
        return lax.rem(z + step + slices, slices) * quad + here

    def sums_copy(zone, g):
        span = pl.ds(g * top, top)
        return pltpu.make_async_remote_copy(
            src_ref=sums_out.at[zone, span],
            dst_ref=sums_in.at[zone, span],
            send_sem=sums_sem.at[0, zone, g],
            recv_sem=sums_sem.at[1, zone, g],
            device_id=device(neighbour(2 * (zone // near) - 1)),
            device_id_type=pl.DeviceIdType.MESH,
        )

    def act_copy(zone):
        return send(
            act_all.at[zone], act_all.at[zone], act_sem, zone, neighbour(1 - 2 * (zone // near))
        )

    def owner(zone):
        return (zone // near) * (slices - 1)

    def source(zone):
        return slices - 1 - owner(zone)

    def marks(zone):
        return routing[pl.ds(zone * quad, quad)].reshape(quad * block, routing.shape[2])

    def relay(zone):
        @pl.when((z != owner(zone)) & (z != source(zone)))
        def _():
            for g in range(2):
                sums_copy(zone, g).wait_recv()
                for k in range(g * top, (g + 1) * top):
                    sums_out[zone, k] = (partial[zone, k] + sums_in[zone, k].astype(f32)).astype(
                        bf16
                    )
                sums_copy(zone, g).start()

    def far_zone(i):
        end = slices - 1
        middle = 1 - z // end - (end - z) // end
        turn = middle * ((i % 2) * near + i // 2) + (1 - middle) * i
        return lax.rem(turn + (1 - z // near) * near, slices)

    def near_zone(i):
        return lax.rem(i + (z // near) * near, slices)

    def up_step(i, carry):
        zone = far_zone(i)
        value = features[pl.ds(zone * quad, quad)].reshape(quad * block, part)
        table = marks(zone)
        for g, matrix in enumerate((gate_ref, up_ref)):
            picked = [jnp.zeros((quad * block, matrix.shape[2]), f32)] * top
            for e in range(experts):
                dense = jnp.dot(value, matrix[e], preferred_element_type=f32)
                for k in range(top):
                    picked[k] = jnp.where(table[:, k : k + 1] == float(e), dense, picked[k])
            for k in range(top):
                partial[zone, g * top + k] = picked[k]

            @pl.when(z == source(zone))
            def _():
                for k in range(g * top, (g + 1) * top):
                    sums_out[zone, k] = partial[zone, k].astype(bf16)
                sums_copy(zone, g).start()

        @pl.when(i > 0)
        def _():
            relay(far_zone(i - 1))

        return carry

    lax.fori_loop(0, slices, up_step, 0)
    relay(far_zone(slices - 1))

    def down_copy(zone, d):
        spot = lax.rem(here + d, quad)
        return pltpu.make_async_remote_copy(
            src_ref=down_out.at[zone, spot],
            dst_ref=down_in.at[zone, here],
            send_sem=down_sem.at[0, zone, d],
            recv_sem=down_sem.at[1, zone, d],
            device_id=device(z * quad + spot),
            device_id_type=pl.DeviceIdType.MESH,
        )

    def down_step(i, carry):
        zone = near_zone(i)

        @pl.when(z == owner(zone))
        def _():
            table = marks(zone)
            for g in range(2):
                sums_copy(zone, g).wait_recv()
            for k in range(top):
                gate = partial[zone, k] + sums_in[zone, k].astype(f32)
                up = partial[zone, top + k] + sums_in[zone, top + k].astype(f32)
                value = gate / (1.0 + jnp.exp(-gate)) * up * table[:, top + k : top + k + 1]
                act_all[zone, k] = value.astype(bf16)

        @pl.when(z != owner(zone))
        def _():
            act_copy(zone).wait_recv()

        @pl.when(z != source(zone))
        def _():
            act_copy(zone).start()

        table = marks(zone)
        total = jnp.zeros((quad * block, part), f32)
        for e in range(experts):
            spread = jnp.zeros(act_all.shape[2:], bf16)
            for k in range(top):
                spread = jnp.where(table[:, k : k + 1] == float(e), act_all[zone, k], spread)
            total = total + lax.dot_general(
                spread, down_ref[e], (((1,), (1,)), ((), ())), preferred_element_type=f32
            )
        down_out[zone] = total.reshape(quad, block, part)
        for d in range(1, quad):
            down_copy(zone, d).start()
        return carry

    lax.fori_loop(0, slices, down_step, 0)

    def settle(zone, carry):
        @pl.when(z != owner(zone))
        def _():
            for g in range(2):
                sums_copy(zone, g).wait_send()

        @pl.when(z != source(zone))
        def _():
            act_copy(zone).wait_send()

        return carry

    lax.fori_loop(0, slices, settle, 0)

    def part_copy(d):
        target = lax.rem(z + d, slices)
        return send(part_out.at[target], part_in.at[z], part_sem, d, target * quad + here)

    for i in range(slices):
        zone = lax.rem(z - i + slices, slices)
        down_in[zone, here] = down_out[zone, here]
        for d in range(1, quad):
            down_copy(zone, d).wait()
        value = down_in[zone, 0]
        for s in range(1, quad):
            value = value + down_in[zone, s]
        part_out[zone] = value
        if i > 0:
            part_copy((slices - i) % slices).start()
    part_in[z] = part_out[z]
    for d in range(1, slices):
        part_copy(d).wait()
    for q in range(slices):
        final[q] = (hidden[q] + part_in[q]).astype(bf16)

    share = slices // halves
    swaps = []
    for d in range(1, halves):
        other = lax.rem(c + d, halves)
        swaps.append(
            send(
                final.at[pl.ds(other * share, share)],
                result_ref.at[c],
                swap_sem,
                d,
                z * quad + x * halves + other,
            )
        )
        swaps[-1].start()
    result_ref[c] = final[pl.ds(c * share, share)]
    for copy in swaps:
        copy.wait()


def move_tokens(
    x_res,
    query_new,
    key_new,
    value_new,
    key_cache,
    value_cache,
    lengths,
    routes,
    route_weight,
    norm_gain,
    out_weight,
    w_gate,
    w_up,
    w_down,
):
    slices = lax.axis_size("expert")
    rows = lax.axis_size("dp")
    halves = lax.axis_size("tensor")
    experts, part, hidden_part = w_gate.shape
    steps, tokens, width = x_res.shape
    top = routes.shape[2]
    mine = steps * tokens
    block = mine // halves
    quad = rows * halves
    count = slices * quad
    share = slices // halves
    f32, bf16 = jnp.float32, jnp.bfloat16

    packed = jnp.concatenate([routes.astype(f32), route_weight], axis=2)
    packed = packed.reshape(halves, block, 2 * top)
    packed = jnp.pad(packed, ((0, 0), (0, 0), (0, 128 - 2 * top)))
    attended = attend_steps(query_new, key_cache, value_cache, key_new, value_new, lengths)
    residual = x_res.reshape(halves, block, slices, part).transpose(0, 2, 1, 3)
    gain = norm_gain.reshape(slices, 1, part)
    per = out_weight.shape[1] // part
    projection = out_weight.reshape(out_weight.shape[0], per, part).transpose(1, 0, 2)
    vmem = pl.BlockSpec(memory_space=pltpu.VMEM)
    anywhere = pl.BlockSpec(memory_space=pl.ANY)
    dma = pltpu.SemaphoreType.DMA
    result = pl.pallas_call(
        functools.partial(layer_kernel, slices, rows, halves, top),
        out_shape=jax.ShapeDtypeStruct((halves, share, block, part), bf16),
        in_specs=[vmem] * 5 + [anywhere] * 3,
        out_specs=vmem,
        scratch_shapes=[
            pltpu.VMEM(w_gate.shape, bf16),
            pltpu.VMEM(w_up.shape, bf16),
            pltpu.VMEM(w_down.shape, bf16),
            pltpu.VMEM((count, block, 128), f32),
            pltpu.VMEM((rows - 1,) + attended.shape, bf16),
            pltpu.VMEM((quad, per, block, part), f32),
            pltpu.VMEM((quad, per, block, part), f32),
            pltpu.VMEM((slices, block, part), f32),
            pltpu.VMEM((slices, block, part), bf16),
            pltpu.VMEM((count, block, part), bf16),
            pltpu.VMEM((slices, 2 * top, quad * block, hidden_part), f32),
            pltpu.VMEM((slices, 2 * top, quad * block, hidden_part), bf16),
            pltpu.VMEM((slices, 2 * top, quad * block, hidden_part), bf16),
            pltpu.VMEM((slices, top, quad * block, hidden_part), bf16),
            pltpu.VMEM((slices, quad, block, part), f32),
            pltpu.VMEM((slices, quad, block, part), f32),
            pltpu.VMEM((slices, block, part), f32),
            pltpu.VMEM((slices, block, part), f32),
            pltpu.VMEM((slices, block, part), bf16),
            dma((3,)),
            dma((2, rows)),
            dma((2, count)),
            dma((2, quad)),
            dma((2, count)),
            dma((2, slices, 2)),
            dma((2, slices)),
            dma((2, slices, quad)),
            dma((2, slices)),
            dma((2, halves)),
        ],
        compiler_params=pltpu.CompilerParams(
            collective_id=0, has_side_effects=True, vmem_limit_bytes=60 * 1024 * 1024
        ),
    )(attended, packed, residual, gain, projection, w_gate, w_up, w_down)
    result = result.transpose(0, 2, 1, 3)
    return result.reshape(steps, tokens, width // halves)


def local(*args):
    x_res, routes, w_gate = args[0], args[7], args[11]
    spread = lax.axis_size("expert") * lax.axis_size("dp")
    travelling = x_res.shape[0] * x_res.shape[1] * spread * routes.shape[2]
    even = lax.axis_size("expert") % 2 == 0
    if even and travelling < w_gate.shape[0] * w_gate.shape[1]:
        return move_tokens(*args)
    return move_weights(*args)


def solution(mesh):
    in_specs = (
        P(None, ("groups", "expert", "dp"), None),
        P(None, ("groups", "expert", "dp"), "tensor"),
        P(None, ("groups", "expert", "dp"), "tensor"),
        P(None, ("groups", "expert", "dp"), "tensor"),
        P(("groups", "expert", "dp"), None, "tensor"),
        P(("groups", "expert", "dp"), None, "tensor"),
        P(("groups", "expert", "dp")),
        P(None, ("groups", "expert", "dp"), None),
        P(None, ("groups", "expert", "dp"), None),
        P(),
        P("tensor", "dp"),
        P(None, "expert", ("dp", "tensor")),
        P(None, "expert", ("dp", "tensor")),
        P(None, "expert", ("dp", "tensor")),
    )
    out_specs = P(None, ("groups", "expert", "dp"), "tensor")
    return jax.shard_map(local, mesh=mesh, in_specs=in_specs, out_specs=out_specs, check_vma=False)
```
